128 devices in a mesh: dp: 64 (over y, z_hi, x, core), head: 2 (over z_lo).
Axes of the slice: x: 4, y: 4, z: 4 (z_hi: 2, z_lo: 2; z = z_hi * 2 + z_lo), core: 2. Of those that a mesh axis runs over, the one named last changes fastest.
Arguments:
- decoder_in: bfloat16 [16384, 768], P('dp'), may hold values from -6 to 6
- encoder_states: bfloat16 [8192, 768], P('dp'), may hold values from -6 to 6
- keep_mask: int32 [8192], P('dp'), may hold values from 0 to 1, as said below
- selection: int32 [16384, 1024], P('dp'), may hold values from 0 to 8191, as said below
- self_proj: bfloat16 [3, 768, 768], P(None, None, 'head'), may hold values from -0.21875 to 0.21875
- self_bias: bfloat16 [2, 768], P(None, 'head'), may hold values from -3 to 3
- self_out: bfloat16 [768, 768], P('head'), may hold values from -1.25 to 1.25
- self_out_bias: bfloat16 [768], replicated, may hold values from -3 to 3
- norm1_gain: bfloat16 [768], replicated, may hold values from 0.5 to 1.5
- norm1_bias: bfloat16 [768], replicated, may hold values from -3 to 3
- cross_query: bfloat16 [768, 768], P(None, 'head'), may hold values from -0.21875 to 0.21875
- cross_memory: bfloat16 [2, 768, 768], P(None, None, 'head'), may hold values from -0.21875 to 0.21875
- cross_bias: bfloat16 [2, 768], P(None, 'head'), may hold values from -3 to 3
- cross_out: bfloat16 [768, 768], P('head'), may hold values from -3.5 to 3.5
- cross_out_bias: bfloat16 [768], replicated, may hold values from -3 to 3
- norm2_gain: bfloat16 [768], replicated, may hold values from 0.5 to 1.5
- norm2_bias: bfloat16 [768], replicated, may hold values from -3 to 3
- expand_weight: bfloat16 [768, 3072], P(None, 'head'), may hold values from -0.21875 to 0.21875
- expand_bias: bfloat16 [3072], P('head'), may hold values from -3 to 3
- reduce_weight: bfloat16 [3072, 768], P('head'), may hold values from -0.109375 to 0.109375
- reduce_bias: bfloat16 [768], replicated, may hold values from -3 to 3
- norm3_gain: bfloat16 [768], replicated, may hold values from 0.5 to 1.5
- norm3_bias: bfloat16 [768], replicated, may hold values from -3 to 3
- out_cotangent: bfloat16 [16384, 768], P('dp'), may hold values from -6 to 6
Outputs:
- layer_out: bfloat16 [16384, 768], P('dp')
- input_grad: float32 [16384, 768], P('dp')
- grad_self_proj: float32 [3, 768, 768], P(None, None, 'head')
- grad_self_bias: float32 [2, 768], P(None, 'head')
- grad_self_out: float32 [768, 768], P('head')
- grad_self_out_bias: float32 [768], replicated
- grad_norm1_gain: float32 [768], replicated
- grad_norm1_bias: float32 [768], replicated
- grad_cross_query: float32 [768, 768], P(None, 'head')
- grad_cross_memory: float32 [2, 768, 768], P(None, None, 'head')
- grad_cross_bias: float32 [2, 768], P(None, 'head')
- grad_cross_out: float32 [768, 768], P('head')
- grad_cross_out_bias: float32 [768], replicated
- grad_norm2_gain: float32 [768], replicated
- grad_norm2_bias: float32 [768], replicated
- grad_expand: float32 [768, 3072], P(None, 'head')
- grad_expand_bias: float32 [3072], P('head')
- grad_reduce: float32 [3072, 768], P('head')
- grad_reduce_bias: float32 [768], replicated
- grad_norm3_gain: float32 [768], replicated
- grad_norm3_bias: float32 [768], replicated
The draws below stay inside these ranges and needn't reach their ends.
Inputs may be any that keep to these rules, and one draw needn't show every extreme that they name: `selection`: each row names 1024 encoder states by their place among all 8192; repeats may occur. Some tokens retrieve only states whose keep_mask is 0. `keep_mask`: each block of 128 consecutive states is one encoder group. Its middle half is kept; its first quarter is kept where a document begins in that group, its last quarter where a document ends there; a document that ends in one group is followed by one that begins in the next. The first group begins a document that goes on into the second group; the last group ends one.
All inputs are finite; a program needn't handle non-finite values.
Results may differ from the reference program's by a relative error of at most 0.035.
Values may be sent and summed in bfloat16 or wider, within the bound.
No kernel may reach another device: no remote copies, remote signals or barrier semaphores. Data moves between devices by JAX's collectives and lax.ppermute only.
A program may use at most 192 MiB of HBM per device.

```python
import jax
import jax.numpy as jnp
from jax import lax

D = 768
HEAD_DIM = 64
FF = 3072
SEQ = 256
ENC_DEV = 128
TOPK = 1024
TOKENS = 16384
STATES = 8192


def group_flags(key):
    blocks = STATES // ENC_DEV
    doc_ends = jax.random.randint(jax.random.fold_in(key, 101), (blocks,), 0, 2)
    doc_ends = doc_ends.at[0].set(0).at[blocks - 1].set(1)
    doc_starts = jnp.concatenate([jnp.ones((1,), jnp.int32), doc_ends[:-1].astype(jnp.int32)])
    return (doc_starts.astype(jnp.int32), doc_ends.astype(jnp.int32))


def draw_keep_mask(key, part):
    doc_starts, doc_ends = group_flags(key)
    quarter = ENC_DEV // 4
    position = jnp.arange(ENC_DEV, dtype=jnp.int32)
    middle = (position >= quarter) & (position < ENC_DEV - quarter)
    head_part = position < quarter
    tail_part = position >= ENC_DEV - quarter
    kept_flags = middle[None, :] | head_part[None, :] & (doc_starts[:, None] == 1) | tail_part[None, :] & (doc_ends[:, None] == 1)
    return kept_flags.reshape(STATES).astype(jnp.int32)


def draw_selection(key, part):
    doc_ends = group_flags(key)[1]
    key = jax.random.fold_in(key, 7)
    subkeys = jax.random.split(key, 10)
    blocks = STATES // ENC_DEV
    shuffled = jax.random.permutation(subkeys[0], blocks)
    upper_block = jax.random.randint(subkeys[1], (TOKENS, TOPK), 0, blocks)
    lower_block = jax.random.randint(subkeys[2], (TOKENS, TOPK), 0, upper_block + 1)
    spread = jax.random.randint(subkeys[3], (TOKENS, TOPK), 0, blocks)
    coin_flip = jax.random.randint(subkeys[4], (TOKENS, TOPK), 0, 2)
    block_index = jnp.where(coin_flip == 1, shuffled[lower_block], spread)
    offset = jax.random.randint(subkeys[5], (TOKENS, TOPK), 0, ENC_DEV)
    picked_rows = block_index * ENC_DEV + offset
    picked_rows = picked_rows.at[0, 0].set(STATES - 1).at[0, 1].set(0)
    sequences = TOKENS // SEQ
    quarter = ENC_DEV // 4
    first_seq = jax.random.randint(subkeys[6], (), 0, sequences)
    second_seq = (first_seq + 1 + jax.random.randint(subkeys[7], (), 0, sequences - 1)) % sequences
    empty_rows = jnp.stack([first_seq, second_seq]) * SEQ + jax.random.randint(subkeys[8], (2,), 1, SEQ)
    empty_block = jax.random.randint(subkeys[9], (2, TOPK), 0, blocks)
    empty_block = jnp.where(doc_ends[empty_block] == 1, 0, empty_block)
    empty_offset = ENC_DEV - quarter + jax.random.randint(jax.random.fold_in(key, 11), (2, TOPK), 0, quarter)
    picked_rows = picked_rows.at[empty_rows].set(empty_block * ENC_DEV + empty_offset)
    return picked_rows.astype(jnp.int32)


def shard_levels(key, shape, cuts, least, top_value):
    def one(axis_at, parts):
        steps = jax.random.uniform(jax.random.fold_in(jax.random.fold_in(key, 6), axis_at), (parts,), jnp.float32, least / len(cuts), top_value / len(cuts))
        return jnp.repeat(jnp.exp(steps), shape[axis_at] // parts).reshape((-1,) + (1,) * (len(shape) - axis_at - 1))

    loudness = one(*cuts[0])
    for cut in cuts[1:]:
        loudness = loudness * one(*cut)
    return loudness


def normal_values(own_key, dims, scale, reach, pieces=(), held_as=jnp.bfloat16):
    factor_of = shard_levels(own_key, dims, pieces, -0.22, 0.18) if pieces else 1.0
    entries = jax.random.normal(own_key, dims, jnp.float32) * scale * factor_of
    return jnp.minimum(jnp.maximum(entries, -reach), reach).astype(held_as)


def setup_inputs(seed: int = 0) -> dict:
    seeds = jax.random.split(jax.random.key(seed), 25)
    decoder_in = normal_values(seeds[0], (TOKENS, D), 1.0, 6.0, ((0, 64),))
    encoder_states = normal_values(seeds[1], (STATES, D), 1.0, 6.0, ((0, 64),))
    keep_mask = draw_keep_mask(jax.random.fold_in(seeds[24], 71), 0)
    selection = draw_selection(jax.random.fold_in(seeds[24], 71), 0)
    self_proj = normal_values(seeds[4], (3, D, D), D ** -0.5, 0.21875, ((2, 2),))
    self_bias = normal_values(seeds[5], (2, D), 0.5, 3.0, ((1, 2),))
    self_out = normal_values(seeds[6], (D, D), (max(D // 32, 1)) ** -0.5, 1.25, ((0, 2),))
    self_out_bias = normal_values(seeds[7], (D,), 0.5, 3.0)
    norm1_gain = jnp.clip(1.0 + 0.1 * jax.random.normal(seeds[8], (D,), jnp.float32), 0.5, 1.5).astype(jnp.bfloat16)
    norm1_bias = normal_values(seeds[9], (D,), 0.2, 3.0)
    cross_query = normal_values(seeds[10], (D, D), D ** -0.5, 0.21875, ((1, 2),))
    cross_memory = normal_values(seeds[11], (2, D, D), D ** -0.5, 0.21875, ((2, 2),))
    cross_bias = normal_values(seeds[12], (2, D), 0.5, 3.0, ((1, 2),))
    cross_out = normal_values(seeds[13], (D, D), (max(D // 256, 1)) ** -0.5, 3.5, ((0, 2),))
    cross_out_bias = normal_values(seeds[14], (D,), 0.5, 3.0)
    norm2_gain = jnp.clip(1.0 + 0.1 * jax.random.normal(seeds[15], (D,), jnp.float32), 0.5, 1.5).astype(jnp.bfloat16)
    norm2_bias = normal_values(seeds[16], (D,), 0.2, 3.0)
    expand_weight = normal_values(seeds[17], (D, FF), D ** -0.5, 0.21875, ((1, 2),))
    expand_bias = normal_values(seeds[18], (FF,), 0.5, 3.0, ((0, 2),))
    reduce_weight = normal_values(seeds[19], (FF, D), FF ** -0.5, 0.109375, ((0, 2),))
    reduce_bias = normal_values(seeds[20], (D,), 0.5, 3.0)
    norm3_gain = jnp.clip(1.0 + 0.1 * jax.random.normal(seeds[21], (D,), jnp.float32), 0.5, 1.5).astype(jnp.bfloat16)
    norm3_bias = normal_values(seeds[22], (D,), 0.2, 3.0)
    out_cotangent = normal_values(seeds[23], (TOKENS, D), 1.0, 6.0, ((0, 64),))
    return {"decoder_in": decoder_in, "encoder_states": encoder_states, "keep_mask": keep_mask, "selection": selection, "self_proj": self_proj, "self_bias": self_bias, "self_out": self_out, "self_out_bias": self_out_bias, "norm1_gain": norm1_gain, "norm1_bias": norm1_bias, "cross_query": cross_query, "cross_memory": cross_memory, "cross_bias": cross_bias, "cross_out": cross_out, "cross_out_bias": cross_out_bias, "norm2_gain": norm2_gain, "norm2_bias": norm2_bias, "expand_weight": expand_weight, "expand_bias": expand_bias, "reduce_weight": reduce_weight, "reduce_bias": reduce_bias, "norm3_gain": norm3_gain, "norm3_bias": norm3_bias, "out_cotangent": out_cotangent}


highest = lax.Precision.HIGHEST
masked_score = -1e+30
epsilon = 1e-05

@jax.custom_vjp
def low(v):
    return lax.optimization_barrier(v.astype(jnp.bfloat16)).astype(jnp.float32)

@jax.custom_vjp
def low_back(v):
    return v

def low_keep(v):
    return (low(v), None)

def low_pass(kept, grad):
    return (grad,)

def back_keep(v):
    return (v, None)

def back_low(kept, grad):
    return (low(grad),)
low.defvjp(low_keep, low_pass)
low_back.defvjp(back_keep, back_low)

def round_both(operand):
    return low(low_back(operand))

def layer_norm(token_rows, norm_gain, norm_bias):
    row_mean = lax.optimization_barrier(jnp.mean(token_rows, axis=-1, keepdims=True))
    centered = token_rows - row_mean
    variance = lax.optimization_barrier(jnp.mean(centered * centered, axis=-1, keepdims=True))
    return centered * lax.rsqrt(variance + epsilon) * norm_gain + norm_bias

def attend(queries, key_rows, value_rows, allowed):
    head_count = queries.shape[1] // HEAD_DIM
    query_heads = queries.reshape(queries.shape[0], head_count, HEAD_DIM)
    key_heads = key_rows.reshape(key_rows.shape[0], head_count, HEAD_DIM)
    value_heads = value_rows.reshape(value_rows.shape[0], head_count, HEAD_DIM)
    scores = jnp.einsum('qhd,khd->hqk', query_heads, key_heads, precision=highest) * HEAD_DIM ** (-0.5)
    scores = low_back(scores)
    scores = jnp.where(allowed[None], scores, masked_score)
    attn_weights = low(jax.nn.softmax(scores, axis=-1))
    mixed = jnp.einsum('hqk,khd->qhd', attn_weights, value_heads, precision=highest)
    return mixed.reshape(queries.shape[0], head_count * HEAD_DIM)

def reference(decoder_in, encoder_states, keep_mask, selection, self_proj, self_bias, self_out, self_out_bias, norm1_gain, norm1_bias, cross_query, cross_memory, cross_bias, cross_out, cross_out_bias, norm2_gain, norm2_bias, expand_weight, expand_bias, reduce_weight, reduce_bias, norm3_gain, norm3_bias, out_cotangent):
    states32 = encoder_states.astype(jnp.float32)
    keep32 = keep_mask.astype(jnp.float32)
    sequences = TOKENS // SEQ
    positions = jnp.arange(SEQ, dtype=jnp.int32)
    causal = positions[:, None] >= positions[None, :]

    def forward(decoder_rows, self_proj, self_bias, self_out, self_out_bias, norm1_gain, norm1_bias, cross_query, cross_memory, cross_bias, cross_out, cross_out_bias, norm2_gain, norm2_bias, expand_weight, expand_bias, reduce_weight, reduce_bias, norm3_gain, norm3_bias):
        key_rows = low(jnp.dot(states32, cross_memory[0], precision=highest))
        value_rows = low(jnp.dot(states32, cross_memory[1], precision=highest) + cross_bias[1])

        def one_sequence(seq_pair):
            token_rows, picked = seq_pair
            projected = jnp.einsum('sd,kde->kse', token_rows, self_proj, precision=highest)
            queries = round_both(projected[0] + self_bias[0])
            self_keys = round_both(projected[1])
            self_values = round_both(projected[2] + self_bias[1])
            self_mixed = round_both(attend(queries, self_keys, self_values, causal))
            after_self = layer_norm(token_rows + low_back(jnp.dot(self_mixed, self_out, precision=highest)) + self_out_bias, norm1_gain, norm1_bias)
            cross_queries = round_both(jnp.dot(low(after_self), cross_query, precision=highest) + cross_bias[0])
            chosen = jnp.zeros((SEQ, STATES), jnp.float32).at[positions[:, None], picked].set(1.0)
            allowed = chosen * keep32[None, :] > 0.5
            recalled = round_both(attend(cross_queries, key_rows, value_rows, allowed))
            after_cross = layer_norm(after_self + low_back(jnp.dot(recalled, cross_out, precision=highest)) + cross_out_bias, norm2_gain, norm2_bias)
            expanded = low_back(jnp.dot(low(after_cross), expand_weight, precision=highest)) + expand_bias
            hidden = round_both(jax.nn.gelu(expanded, approximate=False))
            reduced = low_back(jnp.dot(hidden, reduce_weight, precision=highest)) + reduce_bias
            return layer_norm(after_cross + reduced, norm3_gain, norm3_bias)
        stacked = lax.map(jax.checkpoint(one_sequence), (decoder_rows.reshape(sequences, SEQ, D), selection.reshape(sequences, SEQ, TOPK)))
        return stacked.reshape(TOKENS, D)
    primal, pullback = jax.vjp(forward, decoder_in.astype(jnp.float32), self_proj.astype(jnp.float32), self_bias.astype(jnp.float32), self_out.astype(jnp.float32), self_out_bias.astype(jnp.float32), norm1_gain.astype(jnp.float32), norm1_bias.astype(jnp.float32), cross_query.astype(jnp.float32), cross_memory.astype(jnp.float32), cross_bias.astype(jnp.float32), cross_out.astype(jnp.float32), cross_out_bias.astype(jnp.float32), norm2_gain.astype(jnp.float32), norm2_bias.astype(jnp.float32), expand_weight.astype(jnp.float32), expand_bias.astype(jnp.float32), reduce_weight.astype(jnp.float32), reduce_bias.astype(jnp.float32), norm3_gain.astype(jnp.float32), norm3_bias.astype(jnp.float32))
    gradients = pullback(out_cotangent.astype(jnp.float32))
    return (primal.astype(jnp.bfloat16), gradients[0], gradients[1], gradients[2], gradients[3], gradients[4], gradients[5], gradients[6], gradients[7], gradients[8], gradients[9], gradients[10], gradients[11], gradients[12], gradients[13], gradients[14], gradients[15], gradients[16], gradients[17], gradients[18], gradients[19])
```

```python
import functools

import jax
import jax.numpy as jnp
from jax import lax
from jax.experimental import pallas as pl
from jax.experimental.pallas import tpu as pltpu
from jax.sharding import Mesh
from jax.sharding import PartitionSpec as P

HEAD_DIM = 64
masked_score = -1e30
TOK = 256
HEADS = 6
PAIRS = HEADS // 2
WIDTH = 384
MODEL = 768
SHARD = 128
KEEP_ROWS = 16
PER_BLOCK = 8
BLOCK = SHARD * PER_BLOCK
SEL_TOKENS = 16
CHUNK = 32
ROWS = HEADS * TOK
FIRST = 4 * TOK


SMALL_COST = pl.CostEstimate(flops=2**20, bytes_accessed=2**16, transcendentals=0)


def nt(left, right):
    return lax.dot_general(
        left, right, (((1,), (1,)), ((), ())), preferred_element_type=jnp.float32
    )


def mm(left, right):
    return jnp.dot(left, right, preferred_element_type=jnp.float32)


def table_kernel(sel_ref, *refs):
    out_ref, counts = refs[-2:]
    high_count = out_ref.shape[0]
    picks = sel_ref.shape[1]
    to_low = lambda value: value.astype(jnp.float32).astype(jnp.bfloat16)
    high_rows = to_low(lax.broadcasted_iota(jnp.int32, (high_count, picks), 0))
    low_rows = to_low(lax.broadcasted_iota(jnp.int32, (SHARD, picks), 0))
    one, zero = jnp.bfloat16(1), jnp.bfloat16(0)
    for token in range(SEL_TOKENS):
        row = sel_ref[token : token + 1, :]
        high_hot = jnp.where(high_rows == to_low(row >> 7), one, zero)
        low_hot = jnp.where(low_rows == to_low(row & 127), one, zero)
        counts[pl.ds(token * high_count, high_count), :] = nt(high_hot, low_hot)
    for high in range(high_count):
        rows = counts[pl.ds(high, SEL_TOKENS, stride=high_count), :]
        out_ref[high] = jnp.where(rows > 0.5, 1.0, 0.0).astype(jnp.bfloat16)


def selection_table(selection, high_count, first, count, table):
    tokens, picks = selection.shape
    start = first // SEL_TOKENS
    given = [] if table is None else [table]
    return pl.pallas_call(
        table_kernel,
        grid=(count // SEL_TOKENS,),
        in_specs=[pl.BlockSpec((SEL_TOKENS, picks), lambda i: (i + start, 0))]
        + [pl.BlockSpec(memory_space=pl.ANY)] * len(given),
        out_specs=pl.BlockSpec((high_count, SEL_TOKENS, SHARD), lambda i: (0, i + start, 0)),
        out_shape=jax.ShapeDtypeStruct((high_count, tokens, SHARD), jnp.bfloat16),
        scratch_shapes=[pltpu.VMEM((SEL_TOKENS * high_count, SHARD), jnp.float32)],
        input_output_aliases={1: 0} if given else {},
        compiler_params=pltpu.CompilerParams(vmem_limit_bytes=40 * 2**20),
        cost_estimate=SMALL_COST,
    )(selection, *given)


def lane_tile(tile):
    return slice(tile * SHARD, (tile + 1) * SHARD)


def pair_lanes(pair, start=0):
    first = start + pair * 2 * HEAD_DIM
    return slice(first, first + 2 * HEAD_DIM)


def cross_forward_kernel(fresh, slots, rows_ref, *refs):
    tables = refs[:PER_BLOCK]
    given = refs[PER_BLOCK + 1 : -8]
    query_ref = refs[PER_BLOCK]
    (
        memory_out,
        powers_ref,
        max_ref,
        sum_ref,
        out_ref,
        marks_ref,
        scores_ref,
        mask_ref,
    ) = refs[-8:]

    @pl.when(pl.program_id(0) == 0)
    def _():
        if fresh:
            max_ref[...] = jnp.full_like(max_ref, masked_score)
            sum_ref[...] = jnp.zeros_like(sum_ref)
            out_ref[...] = jnp.zeros_like(out_ref)
            marks_ref[...] = jnp.zeros_like(marks_ref)
        else:
            for ref, before in zip((max_ref, sum_ref, out_ref, marks_ref), given):
                ref[...] = before[...]

    for j in range(PER_BLOCK):
        memory_out[pl.ds(j * SHARD, SHARD), :] = rows_ref[j, :SHARD, :]
        keep_row = rows_ref[j, SHARD : SHARD + KEEP_ROWS, :SHARD].astype(jnp.float32)[0:1, :]
        kept = tables[j][0].astype(jnp.float32) * keep_row
        mask_ref[:, lane_tile(j)] = jnp.where(kept > 0.5, 0.0, masked_score)
    block = slots[slots.shape[0] - 1] + pl.program_id(0)
    here_lane = lax.broadcasted_iota(jnp.int32, (CHUNK, SHARD), 1) == block

    def score(pair):
        rows = pl.ds(pair * 2 * TOK, 2 * TOK)
        scores_ref[pair % 2] = nt(query_ref[rows, :], memory_out[:, pair_lanes(pair)])

    def mix(pair):
        rows = pl.ds(pair * 2 * TOK, 2 * TOK)
        out_ref[rows, :] += mm(powers_ref[rows, :], memory_out[:, pair_lanes(pair, WIDTH)])

    score(0)
    for pair in range(PAIRS):
        if pair + 1 < PAIRS:
            score(pair + 1)
        for first in range(0, 2 * TOK, CHUNK):
            rows = pl.ds(pair * 2 * TOK + first, CHUNK)
            narrow = pl.ds(first, CHUNK)
            token = pl.ds(first % TOK, CHUNK)
            top = scores_ref[pair % 2, narrow, lane_tile(0)] + mask_ref[token, lane_tile(0)]
            for j in range(1, PER_BLOCK):
                tile = scores_ref[pair % 2, narrow, lane_tile(j)] + mask_ref[token, lane_tile(j)]
                top = jnp.maximum(top, tile)
            old_max = max_ref[rows, :]
            new_max = jnp.maximum(old_max, jnp.max(top, axis=1, keepdims=True))
            shrink = jnp.exp(old_max - new_max)
            max_ref[rows, :] = new_max
            sum_ref[rows, :] = sum_ref[rows, :] * shrink
            out_ref[rows, :] = out_ref[rows, :] * shrink
            marks_ref[rows, :] = jnp.where(here_lane, new_max, marks_ref[rows, :])
        for first in range(0, 2 * TOK, CHUNK):
            rows = pl.ds(pair * 2 * TOK + first, CHUNK)
            narrow = pl.ds(first, CHUNK)
            token = pl.ds(first % TOK, CHUNK)
            new_max = max_ref[rows, :]
            total = sum_ref[rows, :]
            for j in range(PER_BLOCK):
                tile = scores_ref[pair % 2, narrow, lane_tile(j)] + mask_ref[token, lane_tile(j)]
                powers = jnp.exp(tile - new_max)
                total = total + powers
                powers_ref[rows, lane_tile(j)] = powers.astype(jnp.bfloat16)
            sum_ref[rows, :] = total
        if pair:
            mix(pair - 1)
    mix(PAIRS - 1)


def whole(*shape):
    return pl.BlockSpec(shape, lambda *_: (0,) * len(shape))


def cross_forward(slots, rows, table, queries, running):
    shard_count = rows.shape[0]
    blocks = shard_count // PER_BLOCK
    states = shard_count * SHARD
    table_spec = lambda j: pl.BlockSpec(
        (1, TOK, SHARD), lambda i, g: (g[PER_BLOCK * i + j], 0, 0)
    )
    stat = jax.ShapeDtypeStruct((ROWS, SHARD), jnp.float32)
    return pl.pallas_call(
        functools.partial(cross_forward_kernel, not running),
        grid_spec=pltpu.PrefetchScalarGridSpec(
            num_scalar_prefetch=1,
            grid=(blocks,),
            in_specs=[
                pl.BlockSpec((PER_BLOCK, SHARD + KEEP_ROWS, MODEL), lambda i, g: (i, 0, 0)),
                *[table_spec(j) for j in range(PER_BLOCK)],
                whole(ROWS, 2 * HEAD_DIM),
                *[whole(ROWS, SHARD)] * len(running),
            ],
            out_specs=[
                pl.BlockSpec((BLOCK, 2 * WIDTH), lambda i, g: (i, 0)),
                pl.BlockSpec((ROWS, BLOCK), lambda i, g: (0, i)),
                *[whole(ROWS, SHARD)] * 4,
            ],
            scratch_shapes=[
                pltpu.VMEM((2, 2 * TOK, BLOCK), jnp.float32),
                pltpu.VMEM((TOK, BLOCK), jnp.float32),
            ],
        ),
        out_shape=[
            jax.ShapeDtypeStruct((states, 2 * WIDTH), jnp.bfloat16),
            jax.ShapeDtypeStruct((ROWS, states), jnp.bfloat16),
            stat,
            stat,
            stat,
            stat,
        ],
        compiler_params=pltpu.CompilerParams(vmem_limit_bytes=56 * 2**20),
        cost_estimate=SMALL_COST,
    )(slots, rows, *([table] * PER_BLOCK), queries, *running)


def cross_backward_kernel(
    fresh,
    base_ref,
    memory_ref,
    powers_ref,
    scale_ref,
    scale_rows_ref,
    upstream_ref,
    turned_query_ref,
    turned_upstream_ref,
    delta_ref,
    *refs,
):
    query_out, bias_out, state_out, grad_ref, change_ref, spread_ref = refs[-6:]

    @pl.when(pl.program_id(0) == 0)
    def _():
        if fresh:
            query_out[...] = jnp.zeros_like(query_out)
            bias_out[...] = jnp.zeros_like(bias_out)
        else:
            query_out[...] = refs[0][...]
            bias_out[...] = refs[1][...]

    block = base_ref[0] + pl.program_id(0)
    here_lane = lax.broadcasted_iota(jnp.int32, (CHUNK, SHARD), 1) == block
    key_start = base_ref[1] * WIDTH
    value_start = (1 - base_ref[1]) * WIDTH
    spots = [
        pl.multiple_of(base_ref[2 + pl.program_id(0) * PER_BLOCK + j] * SHARD, SHARD)
        for j in range(PER_BLOCK)
    ]

    def put(start, grad):
        rows = pl.ds(pl.multiple_of(start, HEAD_DIM), HEAD_DIM)
        for j in range(PER_BLOCK):
            state_out[rows, pl.ds(spots[j], SHARD)] = grad[:, lane_tile(j)].astype(jnp.bfloat16)

    def spread(pair):
        rows = pl.ds(pair * 2 * TOK, 2 * TOK)
        grad_ref[pair % 2] = nt(upstream_ref[rows, :], memory_ref[:, pair_lanes(pair, WIDTH)])

    def finish(pair):
        rows = pl.ds(pair * 2 * TOK, 2 * TOK)
        query_out[rows, :] += mm(change_ref[pair % 2], memory_ref[:, pair_lanes(pair)])
        for side in range(2):
            head = 2 * pair + side
            change = change_ref[pair % 2, side * TOK : (side + 1) * TOK, :]
            key_grad = mm(turned_query_ref[pl.ds(head * HEAD_DIM, HEAD_DIM), :], change)
            put(key_start + head * HEAD_DIM, key_grad)

    spread(0)
    for first in range(0, ROWS, CHUNK):
        rows = pl.ds(first, CHUNK)
        scale = jnp.sum(jnp.where(here_lane, scale_ref[rows, :], 0.0), axis=1, keepdims=True)
        spread_ref[rows, :] = jnp.broadcast_to(scale, (CHUNK, SHARD))
    for pair in range(PAIRS):
        if pair + 1 < PAIRS:
            spread(pair + 1)
        for first in range(0, 2 * TOK, CHUNK):
            rows = pl.ds(pair * 2 * TOK + first, CHUNK)
            narrow = pl.ds(first, CHUNK)
            scale = spread_ref[rows, :]
            delta = delta_ref[rows, :]
            for j in range(PER_BLOCK):
                powers = powers_ref[rows, lane_tile(j)].astype(jnp.float32)
                change = powers * ((grad_ref[pair % 2, narrow, lane_tile(j)] - delta) * scale)
                change_ref[pair % 2, narrow, lane_tile(j)] = change.astype(jnp.bfloat16)
        for head in (2 * pair, 2 * pair + 1):
            narrow = pl.ds(head * HEAD_DIM, HEAD_DIM)
            scaled = turned_upstream_ref[narrow, :] * scale_rows_ref[0, head : head + 1, :]
            value_grad = mm(scaled.astype(jnp.bfloat16), powers_ref[pl.ds(head * TOK, TOK), :])
            put(value_start + head * HEAD_DIM, value_grad)
            total = bias_out[narrow, :]
            for j in range(PER_BLOCK):
                total = total + value_grad[:, lane_tile(j)]
            bias_out[narrow, :] = total
        if pair:
            finish(pair - 1)
    finish(PAIRS - 1)


def cross_backward(base, memory, powers, operands, running):
    states = memory.shape[0]
    blocks = states // BLOCK
    return pl.pallas_call(
        functools.partial(cross_backward_kernel, not running),
        grid_spec=pltpu.PrefetchScalarGridSpec(
            num_scalar_prefetch=1,
            grid=(blocks,),
            in_specs=[
                pl.BlockSpec((BLOCK, 2 * WIDTH), lambda i, b: (i, 0)),
                pl.BlockSpec((ROWS, BLOCK), lambda i, b: (0, i)),
                whole(ROWS, SHARD),
                pl.BlockSpec((1, 8, TOK), lambda i, b: (b[0] + i, 0, 0)),
                whole(ROWS, 2 * HEAD_DIM),
                whole(WIDTH, TOK),
                whole(WIDTH, TOK),
                whole(ROWS, SHARD),
                *[whole(ROWS, SHARD), whole(WIDTH, SHARD)][: len(running)],
            ],
            out_specs=[
                whole(ROWS, SHARD),
                whole(WIDTH, SHARD),
                whole(2 * WIDTH, states),
            ],
            scratch_shapes=[
                pltpu.VMEM((2, 2 * TOK, BLOCK), jnp.float32),
                pltpu.VMEM((2, 2 * TOK, BLOCK), jnp.bfloat16),
                pltpu.VMEM((ROWS, SHARD), jnp.float32),
            ],
        ),
        out_shape=[
            jax.ShapeDtypeStruct((ROWS, SHARD), jnp.float32),
            jax.ShapeDtypeStruct((WIDTH, SHARD), jnp.float32),
            jax.ShapeDtypeStruct((2 * WIDTH, states), jnp.bfloat16),
        ],
        compiler_params=pltpu.CompilerParams(vmem_limit_bytes=56 * 2**20),
        cost_estimate=SMALL_COST,
    )(base, memory, powers, *operands, *running)


epsilon = 1e-05
SCALE = HEAD_DIM ** (-0.5)
LANES2 = 2 * HEAD_DIM


def f32(value):
    return value.astype(jnp.float32)


def low16(value):
    return value.astype(jnp.bfloat16)


def left_side(rows):
    return lax.broadcasted_iota(jnp.int32, (rows, LANES2), 1) < HEAD_DIM


def one_side(pair_rows, head):
    left = left_side(pair_rows.shape[0])
    return jnp.where(left if head % 2 == 0 else ~left, pair_rows, 0.0)


def norm_rows(rows, gain, bias):
    centered = rows - jnp.mean(rows, axis=-1, keepdims=True)
    variance = jnp.mean(centered * centered, axis=-1, keepdims=True)
    inverse = lax.rsqrt(variance + epsilon)
    normed = centered * inverse
    return normed * gain + bias, normed, inverse


def norm_rows_back(upstream, normed, inverse, gain):
    scaled = upstream * gain
    mean_one = jnp.mean(scaled, axis=-1, keepdims=True)
    mean_two = jnp.mean(scaled * normed, axis=-1, keepdims=True)
    return inverse * (scaled - mean_one - normed * mean_two)


def column_sum(rows):
    return jnp.sum(rows, axis=0, keepdims=True)


def gelu_parts(values):
    inner = 0.5 * (1.0 + lax.erf(values * (0.5**0.5)))
    return inner


def dense_call(kernel, outs, *operands):
    shapes = [jax.ShapeDtypeStruct(shape, dtype) for shape, dtype in outs]
    return pl.pallas_call(
        kernel,
        in_specs=[pl.BlockSpec(memory_space=pltpu.VMEM)] * len(operands),
        out_specs=[pl.BlockSpec(memory_space=pltpu.VMEM)] * len(outs),
        out_shape=shapes,
        compiler_params=pltpu.CompilerParams(vmem_limit_bytes=56 * 2**20),
        cost_estimate=SMALL_COST,
    )(*operands)


F = jnp.float32
B = jnp.bfloat16


def self_forward_kernel(x_ref, proj_ref, bias_ref, out_ref, q_ref, k_ref, v_ref, attn_ref, mixed_ref, part_ref):
    x = x_ref[...]
    queries = low16(mm(x, proj_ref[0]) + f32(bias_ref[...])[0:1])
    q_ref[...] = low16(f32(queries) * SCALE)
    k_ref[...] = low16(mm(x, proj_ref[1]))
    v_ref[...] = low16(mm(x, proj_ref[2]) + f32(bias_ref[...])[1:2])
    causal = lax.broadcasted_iota(jnp.int32, (TOK, TOK), 0) >= lax.broadcasted_iota(
        jnp.int32, (TOK, TOK), 1
    )
    left = left_side(TOK)
    for pair in range(PAIRS):
        lanes = pair_lanes(pair)
        mixes = []
        for head in (2 * pair, 2 * pair + 1):
            query = low16(one_side(f32(q_ref[:, lanes]), head))
            scores = jnp.where(causal, nt(query, k_ref[:, lanes]), masked_score)
            powers = jnp.exp(scores - jnp.max(scores, axis=1, keepdims=True))
            attn = powers / jnp.sum(powers, axis=1, keepdims=True)
            attn_ref[head] = attn
            mixes.append(mm(low16(attn), v_ref[:, lanes]))
        mixed_ref[:, lanes] = low16(jnp.where(left, mixes[0], mixes[1]))
    part_ref[...] = low16(mm(mixed_ref[...], out_ref[...]))


def self_forward(x, proj, bias, out_weight):
    return dense_call(
        self_forward_kernel,
        [((TOK, WIDTH), B)] * 3
        + [((HEADS, TOK, TOK), F), ((TOK, WIDTH), B), ((TOK, MODEL), B)],
        x,
        proj,
        bias,
        out_weight,
    )


def first_norm_kernel(x_ref, part_ref, got_ref, rows_ref, weight_ref, bias_ref, after_ref, normed_ref, inverse_ref, low_ref, stack_ref, turned_ref):
    total = f32(x_ref[...]) + (f32(part_ref[...]) + f32(got_ref[...])) + rows_ref[0:1]
    after, normed, inverse = norm_rows(total, rows_ref[1:2], rows_ref[2:3])
    after_ref[...] = after
    normed_ref[...] = normed
    inverse_ref[...] = jnp.broadcast_to(inverse, (TOK, SHARD))
    low_ref[...] = low16(after)
    queries = f32(low16(mm(low_ref[...], weight_ref[...]) + bias_ref[...])) * SCALE
    for head in range(HEADS):
        lanes = pair_lanes(head // 2)
        stack_ref[pl.ds(head * TOK, TOK), :] = low16(one_side(queries[:, lanes], head))
    turned_ref[...] = low16(jnp.transpose(queries))


def first_norm(x, part, got, rows, weight, bias):
    return dense_call(
        first_norm_kernel,
        [
            ((TOK, MODEL), F),
            ((TOK, MODEL), F),
            ((TOK, SHARD), F),
            ((TOK, MODEL), B),
            ((ROWS, LANES2), B),
            ((WIDTH, TOK), B),
        ],
        x,
        part,
        got,
        rows,
        weight,
        bias,
    )


def recall_kernel(mixed_ref, max_ref, sum_ref, marks_ref, weight_ref, full_ref, low_ref, scale_ref, scale_rows_ref, part_ref):
    left = left_side(TOK)
    used = lax.broadcasted_iota(jnp.int32, (TOK, SHARD), 1) < scale_rows_ref.shape[0]
    scale_rows_ref[...] = jnp.zeros_like(scale_rows_ref)
    for pair in range(PAIRS):
        sides = []
        for head in (2 * pair, 2 * pair + 1):
            rows = pl.ds(head * TOK, TOK)
            inverse = 1.0 / jnp.sum(sum_ref[rows, :], axis=1, keepdims=True)
            sides.append(mixed_ref[rows, :] * inverse)
            scales = jnp.where(used, jnp.exp(marks_ref[rows, :] - max_ref[rows, :]) * inverse, 0.0)
            scale_ref[rows, :] = scales
            scale_rows_ref[:, head, :] = jnp.transpose(scales)[: scale_rows_ref.shape[0], :]
        recalled = jnp.where(left, sides[0], sides[1])
        full_ref[:, pair_lanes(pair)] = recalled
        low_ref[:, pair_lanes(pair)] = low16(recalled)
    part_ref[...] = low16(mm(low_ref[...], weight_ref[...]))


def recall(mixed, top, total, marks, weight, blocks):
    return dense_call(
        recall_kernel,
        [
            ((TOK, WIDTH), F),
            ((TOK, WIDTH), B),
            ((ROWS, SHARD), F),
            ((blocks, 8, TOK), F),
            ((TOK, MODEL), B),
        ],
        mixed,
        top,
        total,
        marks,
        weight,
    )


def expand_kernel(after_ref, part_ref, got_ref, rows_ref, expand_ref, bias_ref, reduce_ref, cross_ref, normed_ref, inverse_ref, low_ref, units_ref, hidden_ref, out_ref):
    total = after_ref[...] + (f32(part_ref[...]) + f32(got_ref[...])) + rows_ref[0:1]
    after, normed, inverse = norm_rows(total, rows_ref[1:2], rows_ref[2:3])
    cross_ref[...] = after
    normed_ref[...] = normed
    inverse_ref[...] = jnp.broadcast_to(inverse, (TOK, SHARD))
    low_ref[...] = low16(after)
    units = mm(low_ref[...], expand_ref[...]) + bias_ref[...]
    units_ref[...] = units
    hidden_ref[...] = low16(units * gelu_parts(units))
    out_ref[...] = low16(mm(hidden_ref[...], reduce_ref[...]))


def expand(after, part, got, rows, expand_weight, bias, reduce_weight):
    units = expand_weight.shape[1]
    return dense_call(
        expand_kernel,
        [
            ((TOK, MODEL), F),
            ((TOK, MODEL), F),
            ((TOK, SHARD), F),
            ((TOK, MODEL), B),
            ((TOK, units), F),
            ((TOK, units), B),
            ((TOK, MODEL), B),
        ],
        after,
        part,
        got,
        rows,
        expand_weight,
        bias,
        reduce_weight,
    )


def expand_back_kernel(cross_ref, part_ref, got_ref, rows_ref, upstream_ref, units_ref, expand_ref, reduce_ref, layer_ref, grad_ref, grad_low_ref, units_low_ref, out_ref, sums_ref, unit_sums_ref):
    total = cross_ref[...] + (f32(part_ref[...]) + f32(got_ref[...])) + rows_ref[0:1]
    after, normed, inverse = norm_rows(total, rows_ref[1:2], rows_ref[2:3])
    layer_ref[...] = low16(after)
    upstream = f32(upstream_ref[...])
    grad = norm_rows_back(upstream, normed, inverse, rows_ref[1:2])
    grad_ref[...] = grad
    grad_low_ref[...] = low16(grad)
    sums_ref[...] = jnp.zeros_like(sums_ref)
    sums_ref[0:1, :] = column_sum(grad)
    sums_ref[1:2, :] = column_sum(upstream * normed)
    sums_ref[2:3, :] = column_sum(upstream)
    grad_hidden = f32(low16(nt(grad_low_ref[...], reduce_ref[...])))
    units = units_ref[...]
    density = jnp.exp(-0.5 * units * units) * (0.5 / jnp.pi) ** 0.5
    grad_units = grad_hidden * (gelu_parts(units) + units * density)
    unit_sums_ref[...] = jnp.zeros_like(unit_sums_ref)
    unit_sums_ref[0:1, :] = column_sum(grad_units)
    units_low_ref[...] = low16(grad_units)
    out_ref[...] = low16(nt(units_low_ref[...], expand_ref[...]))


def expand_back(cross, part, got, rows, upstream, units, expand_weight, reduce_weight):
    count = expand_weight.shape[1]
    return dense_call(
        expand_back_kernel,
        [
            ((TOK, MODEL), B),
            ((TOK, MODEL), F),
            ((TOK, MODEL), B),
            ((TOK, count), B),
            ((TOK, MODEL), B),
            ((8, MODEL), F),
            ((8, count), F),
        ],
        cross,
        part,
        got,
        rows,
        upstream,
        units,
        expand_weight,
        reduce_weight,
    )


def second_back_kernel(grad_ref, part_ref, got_ref, rows_ref, normed_ref, inverse_ref, weight_ref, full_ref, max_ref, out_ref, low_ref, sums_ref, stack_ref, turned_ref, delta_ref):
    upstream = grad_ref[...] + (f32(part_ref[...]) + f32(got_ref[...]))
    normed = normed_ref[...]
    grad = norm_rows_back(upstream, normed, inverse_ref[:, 0:1], rows_ref[1:2])
    out_ref[...] = grad
    low_ref[...] = low16(grad)
    sums_ref[...] = jnp.zeros_like(sums_ref)
    sums_ref[0:1, :] = column_sum(grad)
    sums_ref[1:2, :] = column_sum(upstream * normed)
    sums_ref[2:3, :] = column_sum(upstream)
    recalled_grad = f32(low16(nt(low_ref[...], weight_ref[...])))
    turned_ref[...] = jnp.transpose(recalled_grad)
    for head in range(HEADS):
        rows = pl.ds(head * TOK, TOK)
        lanes = pair_lanes(head // 2)
        flags = max_ref[rows, :] > 0.1 * masked_score
        own = one_side(recalled_grad[:, lanes], head)
        delta = jnp.sum(own * full_ref[:, lanes], axis=1, keepdims=True)
        delta_ref[rows, :] = jnp.where(flags, jnp.broadcast_to(delta, (TOK, SHARD)), 0.0)
        stack_ref[rows, :] = low16(jnp.where(flags, own, 0.0))


def second_back(grad, part, got, rows, normed, inverse, weight, full, top):
    return dense_call(
        second_back_kernel,
        [
            ((TOK, MODEL), F),
            ((TOK, MODEL), B),
            ((8, MODEL), F),
            ((ROWS, LANES2), B),
            ((WIDTH, TOK), F),
            ((ROWS, SHARD), F),
        ],
        grad,
        part,
        got,
        rows,
        normed,
        inverse,
        weight,
        full,
        top,
    )


def query_back_kernel(grad_ref, weight_ref, low_ref, part_ref, sums_ref):
    left = left_side(TOK)
    for pair in range(PAIRS):
        first = grad_ref[pl.ds(2 * pair * TOK, TOK), :]
        second = grad_ref[pl.ds((2 * pair + 1) * TOK, TOK), :]
        low_ref[:, pair_lanes(pair)] = low16(jnp.where(left, first, second) * SCALE)
    sums_ref[...] = jnp.zeros_like(sums_ref)
    sums_ref[0:1, :] = column_sum(f32(low_ref[...]))
    part_ref[...] = low16(nt(low_ref[...], weight_ref[...]))


def query_back(grad, weight):
    return dense_call(
        query_back_kernel,
        [((TOK, WIDTH), B), ((TOK, MODEL), B), ((8, WIDTH), F)],
        grad,
        weight,
    )


def self_back_kernel(grad_ref, part_ref, got_ref, rows_ref, normed_ref, inverse_ref, out_weight_ref, q_ref, k_ref, v_ref, attn_ref, proj_ref, out_ref, low_ref, sums_ref, dq_ref, dk_ref, dv_ref, back_ref, bias_ref):
    upstream = grad_ref[...] + (f32(part_ref[...]) + f32(got_ref[...]))
    normed = normed_ref[...]
    grad = norm_rows_back(upstream, normed, inverse_ref[:, 0:1], rows_ref[1:2])
    out_ref[...] = grad
    low_ref[...] = low16(grad)
    sums_ref[...] = jnp.zeros_like(sums_ref)
    sums_ref[0:1, :] = column_sum(grad)
    sums_ref[1:2, :] = column_sum(upstream * normed)
    sums_ref[2:3, :] = column_sum(upstream)
    mixed = low16(nt(low_ref[...], out_weight_ref[...]))
    left = left_side(TOK)
    for pair in range(PAIRS):
        lanes = pair_lanes(pair)
        mixed_pair = mixed[:, lanes]
        query_parts, key_parts, value_parts = [], [], []
        for head in (2 * pair, 2 * pair + 1):
            attn = attn_ref[head]
            grad_attn = nt(low16(one_side(f32(mixed_pair), head)), v_ref[:, lanes])
            center = jnp.sum(attn * grad_attn, axis=1, keepdims=True)
            change = attn * (grad_attn - center)
            change_low = low16(change)
            query_parts.append(mm(change_low, k_ref[:, lanes]))
            key_parts.append(mm(low16(jnp.transpose(f32(change_low))), q_ref[:, lanes]))
            value_parts.append(mm(low16(jnp.transpose(attn)), mixed_pair))
        dq_ref[:, lanes] = low16(jnp.where(left, query_parts[0], query_parts[1]) * SCALE)
        dk_ref[:, lanes] = low16(jnp.where(left, key_parts[0], key_parts[1]))
        dv_ref[:, lanes] = low16(jnp.where(left, value_parts[0], value_parts[1]))
    back = nt(dq_ref[...], proj_ref[0]) + nt(dk_ref[...], proj_ref[1]) + nt(dv_ref[...], proj_ref[2])
    back_ref[...] = low16(back)
    bias_ref[...] = jnp.zeros_like(bias_ref)
    bias_ref[0:1, :] = column_sum(f32(dq_ref[...]))
    bias_ref[1:2, :] = column_sum(f32(dv_ref[...]))


def self_back(grad, part, got, rows, normed, inverse, out_weight, queries, keys, values, attn, proj):
    return dense_call(
        self_back_kernel,
        [
            ((TOK, MODEL), F),
            ((TOK, MODEL), B),
            ((8, MODEL), F),
            ((TOK, WIDTH), B),
            ((TOK, WIDTH), B),
            ((TOK, WIDTH), B),
            ((TOK, MODEL), B),
            ((8, WIDTH), F),
        ],
        grad,
        part,
        got,
        rows,
        normed,
        inverse,
        out_weight,
        queries,
        keys,
        values,
        attn,
        proj,
    )


def finish_kernel(core_ref, mine0_ref, other0_ref, mine1_ref, other1_ref, memory_ref, query_ref, out_ref, proj_ref, self_ref, turned_ref):
    even = core_ref[0] == 0
    rows = MODEL // 32
    for y in range(2):
        for z in range(2):
            for x in range(4):
                at = pl.ds(((y * 2 + z) * 4 + x) * rows, rows)
                first = jnp.where(even, mine0_ref[x, y, z], other0_ref[x, y, z]).astype(F)
                second = jnp.where(even, other1_ref[y, x, z], mine1_ref[y, x, z]).astype(F)
                memory_ref[0, at, :] = first[:rows, :WIDTH]
                query_ref[at, :] = first[:rows, WIDTH:]
                proj_ref[0, at, :] = first[rows : 2 * rows, :WIDTH]
                proj_ref[1, at, :] = first[rows : 2 * rows, WIDTH:]
                memory_ref[1, at, :] = second[:rows, :WIDTH]
                turned_ref[0, at, :] = second[:rows, WIDTH:]
                proj_ref[2, at, :] = second[rows : 2 * rows, :WIDTH]
                turned_ref[1, at, :] = second[rows : 2 * rows, WIDTH:]
    out_ref[...] = jnp.transpose(turned_ref[0])
    self_ref[...] = jnp.transpose(turned_ref[1])


def finish(core, mine, other):
    rows = mine.shape[3]
    first = pl.BlockSpec((4, 2, 2, rows, MODEL), lambda i, c: (0, i, 0, 0, 0))
    second = pl.BlockSpec((2, 4, 2, rows, MODEL), lambda i, c: (i, 0, 0, 0, 0))
    half = MODEL // 2
    return pl.pallas_call(
        finish_kernel,
        grid_spec=pltpu.PrefetchScalarGridSpec(
            num_scalar_prefetch=1,
            grid=(2,),
            in_specs=[first, first, second, second],
            out_specs=[
                pl.BlockSpec((2, half, WIDTH), lambda i, c: (0, i, 0)),
                pl.BlockSpec((half, WIDTH), lambda i, c: (i, 0)),
                pl.BlockSpec((WIDTH, half), lambda i, c: (0, i)),
                pl.BlockSpec((3, half, WIDTH), lambda i, c: (0, i, 0)),
                pl.BlockSpec((WIDTH, half), lambda i, c: (0, i)),
            ],
            scratch_shapes=[pltpu.VMEM((2, half, WIDTH), F)],
        ),
        out_shape=[
            jax.ShapeDtypeStruct((2, MODEL, WIDTH), F),
            jax.ShapeDtypeStruct((MODEL, WIDTH), F),
            jax.ShapeDtypeStruct((WIDTH, MODEL), F),
            jax.ShapeDtypeStruct((3, MODEL, WIDTH), F),
            jax.ShapeDtypeStruct((WIDTH, MODEL), F),
        ],
        compiler_params=pltpu.CompilerParams(vmem_limit_bytes=56 * 2**20),
        cost_estimate=SMALL_COST,
    )(core, mine, other, mine, other)


RING = 4


def place(y, z, x, core):
    return (((y % RING) * 2 + z % 2) * RING + x % RING) * 2 + core % 2


def every_place():
    return [
        (y, z, x, core)
        for y in range(RING)
        for z in range(2)
        for x in range(RING)
        for core in range(2)
    ]


def here():
    return tuple(lax.axis_index(name) for name in DP)


DP = ("y", "z", "x", "core")


def partner(level, y, z, x, core):
    if level == "core":
        return y, z, x, 1 - core
    if level == "depth":
        return y, 1 - z, x, core
    flip = 1 if level[1] == "1" else 3
    if (level[0] == "a") == (core == 0):
        return y, z, x ^ flip, core
    return y ^ flip, z, x, core


def exchange(array, level):
    pairs = [(place(*at), place(*partner(level, *at))) for at in every_place()]
    return lax.ppermute(array, DP, pairs)


def swap_depth(array):
    pairs = []
    for y, z, x, core in every_place():
        for head in range(2):
            pairs.append(
                (place(y, z, x, core) * 2 + head, place(y, z + 1, x, core) * 2 + 1 - head)
            )
    return lax.ppermute(array, DP + ("head",), pairs)


def project(states, keep_rows, weights, bias_row):
    memory = jnp.dot(states, weights, preferred_element_type=jnp.float32) + bias_row
    return jnp.concatenate([memory.astype(jnp.bfloat16), keep_rows], axis=0)


def gather_plane(shard):
    return lax.all_gather(shard, ("y", "x"), axis=0, tiled=True)


def core_slots(depth, side):
    return jnp.stack([place(a, depth, b, side) for a in range(RING) for b in range(RING)])


def far_slots(depth, side):
    y, z, x, core = here()
    steps = [(a, b) for a in range(RING) for b in range(RING)]
    first = jnp.stack([place(y + b, depth, x + a, 0) for a, b in steps])
    second = jnp.stack([place(y + a, depth, x + b, 1) for a, b in steps])
    return jnp.where(side == 0, first, second)


def rounded(rows):
    return lax.reduce_precision(rows, 8, 7)


def two_terms(rows):
    high = rounded(rows)
    low = rounded(rows - high)
    return jnp.concatenate([high, low], axis=0).astype(jnp.bfloat16)


def one_term(rows):
    count = rows.shape[0] // 2
    return rows[:count].astype(jnp.float32) + rows[count:].astype(jnp.float32)


CHIPS = ("y", "z", "x")
CHIP_COUNT = RING * RING * 2
EXTRA_ROWS = 8


def reduce_chips(totals, extra):
    lanes = totals[0].shape[1]
    chunks = [total.astype(jnp.bfloat16).reshape(CHIP_COUNT, -1, lanes) for total in totals]
    if extra is not None:
        terms = two_terms(extra.reshape(CHIP_COUNT, -1)).reshape(2, CHIP_COUNT, -1)
        terms = jnp.concatenate([terms[0], terms[1]], axis=1)[:, None, :]
        filler = jnp.zeros((CHIP_COUNT, EXTRA_ROWS - 1, lanes), jnp.bfloat16)
        chunks += [terms, filler]
    return lax.all_to_all(jnp.concatenate(chunks, axis=1), CHIPS, 0, 0, tiled=True)


def chip_sum(chunks):
    return jnp.sum(chunks.astype(jnp.float32), axis=0)


def move_axis(array, which, step):
    pairs = []
    for y, z, x, core in every_place():
        if (which == "a") == (core == 0):
            to = place(y, z, x + step, core)
        else:
            to = place(y + step, z, x, core)
        pairs.append((place(y, z, x, core), to))
    return lax.ppermute(array, DP, pairs)


def spread_ring(piece, which):
    y, z, x, core = here()
    spot = jnp.where((core == 0) == (which == "a"), x, y)
    got = [piece] + [move_axis(piece, which, -step) for step in (1, 2, 3)]
    ordered = []
    for chunk in range(RING):
        step = (chunk - spot) % RING
        near = jnp.where(step == 0, got[0], got[1])
        ordered.append(jnp.where(step < 2, near, jnp.where(step == 2, got[2], got[3])))
    return jnp.stack(ordered)


def spread_depth(piece):
    z = lax.axis_index("z")
    other = exchange(piece, "depth")
    return jnp.where(z == 0, jnp.stack([piece, other]), jnp.stack([other, piece]))


def by_core(mine, even):
    other = exchange(mine, "core")
    return jnp.where(even, mine, other), jnp.where(even, other, mine)


def turned_dot(left, right):
    return jnp.einsum("sd,se->de", left, right, preferred_element_type=jnp.float32)


def own_and_sent(even, left, right, other_left, other_right):
    mine = turned_dot(jnp.where(even, left, other_left), jnp.where(even, right, other_right))
    sent = turned_dot(jnp.where(even, other_left, left), jnp.where(even, other_right, right))
    return mine, sent.astype(jnp.bfloat16)


def swap_heads(part):
    return lax.ppermute(part, "head", [(0, 1), (1, 0)])


def three_rows(*rows):
    rows = [row.astype(jnp.float32)[None] for row in rows]
    return jnp.concatenate(rows + [jnp.zeros((8 - len(rows), rows[0].shape[1]))], axis=0)


def shards(
    decoder_in,
    encoder_states,
    keep_mask,
    selection,
    self_proj,
    self_bias,
    self_out,
    self_out_bias,
    norm1_gain,
    norm1_bias,
    cross_query,
    cross_memory,
    cross_bias,
    cross_out,
    cross_out_bias,
    norm2_gain,
    norm2_bias,
    expand_weight,
    expand_bias,
    reduce_weight,
    reduce_bias,
    norm3_gain,
    norm3_bias,
    out_cotangent,
):
    even = lax.axis_index("core") == 0
    core = lax.axis_index("core")
    depth = lax.axis_index("z")
    barrier = lax.optimization_barrier
    tie = lambda value, other: barrier((value, other))[0]

    cross_rows = cross_bias.astype(jnp.float32)
    bias_row = jnp.concatenate([jnp.zeros((1, WIDTH), jnp.float32), cross_rows[1:2]], axis=1)
    memory_weights = jnp.concatenate([cross_memory[0], cross_memory[1]], axis=1)
    keep_rows = jnp.zeros((KEEP_ROWS, MODEL), jnp.bfloat16)
    keep_rows = keep_rows.at[0, :SHARD].set(keep_mask.astype(jnp.bfloat16))
    far = swap_depth(jnp.concatenate([encoder_states, keep_rows], axis=0))
    near_rows = gather_plane(project(encoder_states, keep_rows, memory_weights, bias_row))

    queries, keys, values, attn, mixed_low, part = self_forward(
        decoder_in, self_proj, self_bias, self_out
    )
    got = swap_heads(part)
    far, selection = barrier((far, selection, part))[:2]
    far_states = far[:SHARD]
    far_rows = project(far_states, far[SHARD:], memory_weights, bias_row)
    far_row = [far_rows] + [move_axis(far_rows, "b", -step) for step in (1, 2, 3)]
    table = selection_table(selection, 64, 0, TOK, None)
    got, far_row, table = barrier((got, far_row, table))
    far_row = jnp.concatenate(far_row, axis=0)
    far_rows = [far_row] + [move_axis(far_row, "a", -step) for step in (1, 2, 3)]
    norm1_rows = three_rows(self_out_bias, norm1_gain, norm1_bias)
    after_self, normed1, inverse1, after_self_low, query_stack, turned_queries = first_norm(
        decoder_in, part, got, norm1_rows, cross_query, cross_rows[0:1]
    )

    running = ()
    kept = []
    block = 0
    near_rows, table = barrier((near_rows, table))
    for at in (depth, 1 - depth):
        if block:
            far_rows = barrier((far_rows, near_stats))[0]
            mine, order = jnp.concatenate(far_rows, axis=0), far_slots
        else:
            mine, order = near_rows, core_slots
        for side, rows in ((core, mine), (1 - core, exchange(mine, "core"))):
            slots = order(at, side)
            bases = jnp.concatenate([slots, jnp.full((1,), block, slots.dtype)])
            memory, powers, *running = cross_forward(
                bases,
                rows.reshape(slots.shape[0], SHARD + KEEP_ROWS, MODEL),
                table,
                query_stack,
                running,
            )
            spots = ((slots // 16) * RING + (slots // 2) % RING).astype(jnp.int32)
            kept.append((block, spots, memory, powers))
            if block == 0:
                near_stats = running[1][:1]
                near_states, far_states, _ = barrier((encoder_states, far_states, near_stats))
                near_states = gather_plane(near_states)
                far_states = gather_plane(far_states)
            block += slots.shape[0] // PER_BLOCK
    top, total, mixed, marks = running
    recalled_full, recalled, scales, scale_rows, part = recall(
        mixed, top, total, marks, cross_out, block
    )
    norm2_rows = three_rows(cross_out_bias, norm2_gain, norm2_bias)
    after_cross, normed2, inverse2, after_cross_low, units, hidden, part = expand(
        after_self,
        part,
        swap_heads(part),
        norm2_rows,
        expand_weight,
        expand_bias.astype(jnp.float32)[None],
        reduce_weight,
    )
    norm3_rows = three_rows(reduce_bias, norm3_gain, norm3_bias)
    layer_out, grad_r3, grad_r3_low, units_low, part, sums3, unit_sums = expand_back(
        after_cross,
        part,
        swap_heads(part),
        norm3_rows,
        out_cotangent,
        units,
        expand_weight,
        reduce_weight,
    )
    got = swap_heads(part)

    half_units = units_low.shape[1] // 2
    wide_keep, wide_sent = [], []
    for lanes in (slice(0, half_units), slice(half_units, 2 * half_units)):
        mine, sent = own_and_sent(
            even, hidden[:, lanes], grad_r3_low, after_cross_low, units_low[:, lanes]
        )
        wide_keep.append(mine)
        wide_sent.append(sent)
    wide = jnp.concatenate(wide_keep, axis=0) + exchange(
        jnp.concatenate(wide_sent, axis=0), "core"
    ).astype(jnp.float32)
    wide = wide.astype(jnp.bfloat16)

    grad_r2, grad_r2_low, sums2, upstream_stack, turned_upstream, delta = second_back(
        grad_r3, part, got, norm2_rows, normed2, inverse2, cross_out, recalled_full, top
    )
    upstream_stack, wide = barrier((upstream_stack, wide))
    wide = reduce_chips([wide], None)
    operands = (scales, scale_rows, upstream_stack, turned_queries, turned_upstream, delta)
    back = ()
    state_grads = []
    for base, spots, memory, powers in kept:
        heading = jnp.concatenate([jnp.stack([jnp.int32(base), core]), spots])
        *back, state_grad = cross_backward(heading, memory, powers, operands, back)
        state_grads.append(state_grad)
        if len(state_grads) == 2:
            near_states, back = barrier((near_states, back))
            near_pair = [near_states, exchange(near_states, "core")]
    wide, back = barrier((wide, back))
    wide = chip_sum(wide).astype(jnp.bfloat16)
    query_grad, value_bias_grad = back
    query_low, part, query_sums = query_back(query_grad, cross_query)
    got = swap_heads(part)

    def state_products(states, state_grads):
        total = 0.0
        for rows, state_grad in zip(states, state_grads):
            total = total + jnp.einsum(
                "ed,ke->dk", rows, state_grad, preferred_element_type=jnp.float32
            )
        return total

    near_pair, wide, part = barrier((near_pair, wide, part))
    wide = gather_plane(spread_depth(wide)[None])
    memory_grad = state_products(near_pair, state_grads[:2])
    got, memory_grad = barrier((got, memory_grad))
    grad_r1, grad_r1_low, sums1, grad_q, grad_k, grad_v, part, self_sums = self_back(
        grad_r2,
        part,
        got,
        norm1_rows,
        normed1,
        inverse1,
        self_out,
        queries,
        keys,
        values,
        attn,
        self_proj,
    )
    mine, sent = own_and_sent(even, decoder_in, grad_q, decoder_in, grad_v)
    mine_two, sent_two = own_and_sent(even, decoder_in, grad_k, grad_r1_low, mixed_low)
    self_keep = jnp.concatenate([mine, mine_two], axis=1)
    small = [
        self_sums[:2].reshape(1, MODEL),
        sums1[:3],
        jnp.concatenate([query_sums[:1], jnp.sum(value_bias_grad, axis=1)[None]], axis=1),
        sums2[:3],
        unit_sums[:1].reshape(2, MODEL),
        sums3[:3],
        jnp.zeros((3, MODEL), jnp.float32),
    ]
    terms = two_terms(jnp.concatenate(small, axis=0))
    self_sent = jnp.concatenate([sent, sent_two, ], axis=1)
    self_sent = jnp.concatenate([self_sent, terms], axis=0)
    got = exchange(self_sent, "core")
    input_grad = grad_r1 + (part.astype(jnp.float32) + swap_heads(part).astype(jnp.float32))

    far_states, self_sent = barrier((far_states, self_sent))
    far_pair = [far_states, exchange(far_states, "core")]
    memory_grad = memory_grad + state_products(far_pair, state_grads[2:])
    mine, sent = own_and_sent(even, after_self_low, query_low, grad_r2_low, recalled)
    cross_keep = jnp.concatenate([memory_grad[:, :WIDTH], mine], axis=1)
    cross_sent = jnp.concatenate([memory_grad[:, WIDTH:].astype(jnp.bfloat16), sent], axis=1)
    cross_got = exchange(cross_sent, "core")
    small = one_term(terms) + one_term(got[MODEL:])
    self_total = self_keep + got[:MODEL].astype(jnp.float32)
    cross_total = cross_keep + cross_got.astype(jnp.float32)
    cross_total, self_total, small, input_grad = barrier(
        (cross_total, self_total, small, input_grad)
    )
    chunks = reduce_chips([cross_total, self_total], small)

    rows = MODEL // CHIP_COUNT
    both_sum = chip_sum(chunks)
    lanes = MODEL // 2
    small = both_sum[2 * rows : 2 * rows + 1]
    small = two_terms(small[:, :lanes] + small[:, lanes:])
    piece = jnp.concatenate(
        [
            both_sum[: 2 * rows].astype(jnp.bfloat16),
            jnp.concatenate([small[:1], small[1:]], axis=1),
            jnp.zeros((EXTRA_ROWS - 1, MODEL), jnp.bfloat16),
        ],
        axis=0,
    )
    piece = spread_depth(piece)
    piece = spread_ring(piece, "b")
    wide, piece = barrier((wide, piece))
    wide = jnp.transpose(wide.reshape(RING, RING, 2, -1, MODEL), (0, 2, 1, 3, 4))
    five, six = by_core(wide.reshape(2 * MODEL, MODEL), even)
    grad_reduce = five.astype(jnp.float32)
    grad_expand = jnp.concatenate([six[:MODEL], six[MODEL:]], axis=1).astype(jnp.float32)
    mine = spread_ring(piece, "a")
    other = exchange(mine, "core")
    grad_cross_memory, grad_cross_query, grad_cross_out, grad_self_proj, grad_self_out = finish(
        core[None].astype(jnp.int32), mine, other
    )
    small = jnp.where(even, mine[:, :, :, 2 * rows], other[:, :, :, 2 * rows])
    small = jnp.transpose(small, (1, 2, 0, 3)).reshape(CHIP_COUNT, MODEL).astype(jnp.float32)
    small = (small[:, :lanes] + small[:, lanes:]).reshape(-1, MODEL)
    return (
        layer_out,
        input_grad,
        grad_self_proj,
        small[0].reshape(2, WIDTH),
        grad_self_out,
        small[1],
        small[2],
        small[3],
        grad_cross_query,
        grad_cross_memory,
        small[4].reshape(2, WIDTH),
        grad_cross_out,
        small[5],
        small[6],
        small[7],
        grad_expand,
        small[8:10].reshape(-1),
        grad_reduce,
        small[10],
        small[11],
        small[12],
    )


def solution(mesh):
    in_specs = (
        P(DP, None),
        P(DP, None),
        P(DP),
        P(DP, None),
        P(None, None, "head"),
        P(None, "head"),
        P("head", None),
        P(),
        P(),
        P(),
        P(None, "head"),
        P(None, None, "head"),
        P(None, "head"),
        P("head", None),
        P(),
        P(),
        P(),
        P(None, "head"),
        P("head"),
        P("head", None),
        P(),
        P(),
        P(),
        P(DP, None),
    )
    out_specs = (
        P(DP, None),
        P(DP, None),
        P(None, None, "head"),
        P(None, "head"),
        P("head", None),
        P(),
        P(),
        P(),
        P(None, "head"),
        P(None, None, "head"),
        P(None, "head"),
        P("head", None),
        P(),
        P(),
        P(),
        P(None, "head"),
        P("head"),
        P("head", None),
        P(),
        P(),
        P(),
    )
    grid = Mesh(mesh.devices.reshape(RING, 2, RING, 2, 2), DP + ("head",))
    return jax.shard_map(shards, mesh=grid, in_specs=in_specs, out_specs=out_specs, check_vma=False)
```
